512 devices in a mesh: segment: 16 (over z_lo, x), row: 32 (over z_hi, y, core).
Axes of the slice: x: 4, y: 8, z: 8 (z_hi: 2, z_lo: 4; z = z_hi * 4 + z_lo), core: 2. Of those that a mesh axis runs over, the one named last changes fastest.
Arguments:
- input_fields: float32 [4, 32, 32, 4, 256], P(None, 'row'), may hold values from -6 to 6
- injection_order: int32 [4], replicated, may hold values from 0 to 3, each once
- dispersion: float32 [16, 768, 256], P('segment'), may hold values from -0.21875 to 0.21875
- coupling: float32 [16, 4, 32, 32], P('segment', None, 'row'), may hold values from 0.03 to 0.2
- amplifier_gain: float32 [16, 32, 32], P('segment', 'row'), may hold values from 0.4 to 1.6
- inversion: float32 [16, 32, 32], P('segment', 'row'), may hold values from 0.3 to 1
Outputs:
- tap_fields: float32 [16, 4, 32, 32, 4, 256], P('segment', None, 'row')
The draws below stay inside these ranges and needn't reach their ends.
Inputs may be any that keep to these rules, and one draw needn't show every extreme that they name: `injection_order`: each realization enters exactly once.
All inputs are finite; a program needn't handle non-finite values.
Results may differ from the reference program's by a relative error of at most 0.00018.
Values sent between devices are 32-bit elements; how exact they have to be, the bound alone decides.
No kernel may reach another device: no remote copies, remote signals or barrier semaphores. Data moves between devices by JAX's collectives and lax.ppermute only.
A program may use at most 64 MiB of HBM per device.

```python
import math
import jax
import jax.numpy as jnp
from jax import lax

LROWS = 32
LCOLS = 32
BLK = 128
TW = 512
R = 4
STEPS = 2
NSEC = 16
NB = 4


def level_of(rng, shape, split, least, largest):
    loudness, own = 1.0, jax.random.fold_in(rng, 6)
    for axis_at, parts in split:
        draws = jnp.exp(jax.random.uniform(jax.random.fold_in(own, axis_at), (parts,), jnp.float32, least / len(split), largest / len(split)))
        loudness = loudness * jnp.repeat(draws, shape[axis_at] // parts).reshape([-1 if axis == axis_at else 1 for axis in range(len(shape))])
    return loudness


def scatter_about(stream_key, extent, deviation, limit, split=(), dtype=jnp.bfloat16):
    gain = level_of(stream_key, extent, split, -0.22, 0.18) if split else 1.0
    result = jax.random.normal(stream_key, extent, jnp.float32) * deviation * gain
    return jnp.minimum(jnp.maximum(result, -limit), limit).astype(dtype)


def setup_inputs(seed: int = 0) -> dict:
    splits = jax.random.split(jax.random.key(seed), 7)
    return {
        "input_fields": scatter_about(splits[0], (R, LROWS, LCOLS, NB, 2 * BLK), 1.0, 6.0, ((1, 32),), jnp.float32),
        "injection_order": jax.random.permutation(splits[1], R).astype(jnp.int32),
        "dispersion": scatter_about(splits[2], (NSEC, 6 * BLK, 2 * BLK), (6 * BLK) ** -0.5, 0.21875, ((0, 16),), jnp.float32),
        "coupling": jnp.clip(jnp.exp(math.log(0.2) - 1.89712 * jax.random.uniform(splits[3], (NSEC, 4, LROWS, LCOLS), jnp.float32) ** level_of(splits[3], (NSEC, 4, LROWS, LCOLS), ((0, 16), (2, 32)), -0.2, 0.2)), 0.03, 0.2),
        "amplifier_gain": jnp.clip(jnp.exp(math.log(1.6) - 1.3862944 * jax.random.uniform(splits[4], (NSEC, LROWS, LCOLS), jnp.float32) ** level_of(splits[4], (NSEC, LROWS, LCOLS), ((0, 16), (1, 32)), -0.2, 0.2)), 0.4, 1.6),
        "inversion": jnp.clip(0.3 + 0.7 * jax.random.uniform(splits[5], (NSEC, LROWS, LCOLS), jnp.float32) ** level_of(splits[5], (NSEC, LROWS, LCOLS), ((0, 16), (1, 32)), -0.2, 0.2), 0.3, 1.0),
    }


saturation_power = 1.0
loss_rate = 0.2
recovery = 0.8


def kernel_of(section_matrix):
    span = section_matrix.shape[1]
    return jnp.concatenate([section_matrix[0:span], section_matrix[span:2 * span], section_matrix[2 * span:3 * span]], axis=1)


def advance(extended, kernel, bonds, gain_now, inversion_now, samples):
    own_rows = extended[1:-1]
    block_width = own_rows.shape[-1]
    leading = own_rows.shape[:-1]
    mixed = jnp.dot(own_rows.reshape(-1, block_width), kernel, precision=lax.Precision.HIGHEST)
    mixed = mixed.reshape(leading + (3 * block_width,))
    before = mixed[..., :block_width]
    middle = mixed[..., block_width:2 * block_width]
    following = mixed[..., 2 * block_width:]
    zero_block = jnp.zeros_like(before[:, :, :1])
    dispersed = middle + jnp.concatenate([zero_block, before[:, :, :-1]], axis=2) + jnp.concatenate([following[:, :, 1:], zero_block], axis=2)
    padded = jnp.pad(own_rows, ((0, 0), (1, 1), (0, 0), (0, 0)))
    spread = bonds[0][:, :, None, None] * extended[:-2] + bonds[1][:, :, None, None] * extended[2:] + bonds[2][:, :, None, None] * padded[:, :-2] + bonds[3][:, :, None, None] * padded[:, 2:]
    half_width = block_width // 2
    turned = jnp.concatenate([-spread[..., half_width:], spread[..., :half_width]], axis=-1)
    linear = dispersed + turned
    mean_power = jnp.sum(linear * linear, axis=(2, 3)) / samples
    factor = jnp.exp(0.5 * (gain_now * inversion_now / (1.0 + mean_power / saturation_power) - loss_rate))
    return factor[:, :, None, None] * linear


def reference(input_fields, injection_order, dispersion, coupling, amplifier_gain, inversion):
    inversion_now = inversion
    outputs = []
    for slot_number in range(R):
        current = jnp.take(input_fields, injection_order[slot_number], axis=0)
        per_section = []
        for section in range(NSEC):
            kernel = kernel_of(dispersion[section])
            for step_number in range(STEPS):
                extended = jnp.pad(current, ((1, 1), (0, 0), (0, 0), (0, 0)))
                current = advance(extended, kernel, coupling[section], amplifier_gain[section], inversion_now[section], TW)
            mean_power = jnp.sum(current * current, axis=(2, 3)) / TW
            updated = 1.0 - recovery * (1.0 - inversion_now[section] / (1.0 + mean_power / saturation_power))
            inversion_now = inversion_now.at[section].set(updated)
            per_section.append(current)
        outputs.append(jnp.stack(per_section))
    return jnp.stack(outputs, axis=1)
```

```python
import functools

import jax
import jax.numpy as jnp
from jax import lax
from jax.experimental import pallas as pl
from jax.experimental.pallas import tpu as pltpu
from jax.sharding import PartitionSpec as P

STEPS = 2
loss_rate = 0.2
recovery = 0.8
F32 = jnp.float32
BF16 = jnp.bfloat16

ROWS = 16
GROUP = 4
LAG = 2


def section_kernel(
    turn, blocks, info, e_in, halo, msg, coef, *rest
):
    w_refs = rest[:blocks]
    taps_in, e_out, pay, taps_out, mid, w_f32, w_hi, w_lo, w_sem, t_sem = rest[blocks:]
    active = info[0]
    slot = info[1]
    block = info[2]
    first = info[3]
    core = info[4]
    keep = info[5]
    keep_row = info[6]
    lane = lax.broadcasted_iota(jnp.int32, (32, 128), 1)
    other = 1 - core

    @pl.when(active == 0)
    def _():
        e_out[...] = e_in[...]
        pay[0:128, :] = e_in[ROWS - 1].reshape(128, 256)
        pay[128:256, :] = e_in[ROWS - 2].reshape(128, 256)
        pay[256:288, :] = jnp.zeros((32, 256), F32)

    @pl.when(active == 1)
    def _():
        for k in range(blocks):

            @pl.when(block == k)
            def _(k=k):
                copy = pltpu.make_async_copy(w_refs[k].at[:, slot], w_f32, w_sem)
                copy.start()
                copy.wait()

        w = w_f32[...].reshape(768, 256)
        hi = w.astype(BF16)
        w_hi[...] = hi
        w_lo[...] = (w - hi.astype(F32)).astype(BF16)

        theirs = pltpu.roll(msg[other, :, 0:128], 1, 1)
        received = jnp.where(lane == ROWS, theirs, msg[core, :, 0:128])
        n = jnp.where(first == 1, coef[0], received)
        gain_n = coef[1] * n

        def products(x):
            rows = x.shape[0]
            flat = x.reshape(rows * 4, 32, 256)
            hi = flat.astype(BF16)
            lo = (flat - hi.astype(F32)).astype(BF16)
            zero = jnp.zeros((32, 256), BF16)

            def wide(v):
                parts = []
                for i in range(rows * 4):
                    b = i % 4
                    before = v[i - 1] if b > 0 else zero
                    after = v[i + 1] if b < 3 else zero
                    parts.append(jnp.concatenate([before, v[i], after], axis=1))
                return jnp.concatenate(parts, axis=0)

            hi, lo = wide(hi), wide(lo)
            y = jnp.dot(hi, w_hi[...], preferred_element_type=F32)
            y += jnp.dot(lo, w_hi[...], preferred_element_type=F32)
            y += jnp.dot(hi, w_lo[...], preferred_element_type=F32)
            return y.reshape(rows, 4, 32, 256)

        def rows_step(get, get_next, put, base, count, last_n):
            static = isinstance(base, int)
            turn_by = (128 - base) % 128 if static else lax.rem(128 - base, 128)
            gn = pltpu.roll(gain_n, turn_by, 1)
            c_prev = pltpu.roll(coef[2], turn_by, 1)
            c_next = pltpu.roll(coef[3], turn_by, 1)
            c_left = pltpu.roll(coef[4], turn_by, 1)
            c_right = pltpu.roll(coef[5], turn_by, 1)
            n_here = pltpu.roll(n, turn_by, 1)
            x = get(base, count)
            y = products(x)
            for r in range(count):
                before = get(max(base - 1, 0) if static else jnp.maximum(base - 1, 0), 1)[0] if r == 0 else x[r - 1]
                after = get_next() if r == count - 1 else x[r + 1]
                cp, cn = c_prev[:, r : r + 1], c_next[:, r : r + 1]
                cl, cr = c_left[:, r : r + 1], c_right[:, r : r + 1]
                linear = []
                power = jnp.zeros((32, 128), F32)
                for b in range(4):
                    own = x[r, b]
                    spread = (
                        cp * before[b]
                        + cn * after[b]
                        + cl * pltpu.roll(own, 1, 0)
                        + cr * pltpu.roll(own, 31, 0)
                    )
                    re = y[r, b, :, 0:128] - spread[:, 128:256]
                    im = y[r, b, :, 128:256] + spread[:, 0:128]
                    power += re * re + im * im
                    linear.append((re, im))
                mean = jnp.sum(power, axis=1, keepdims=True) * (1.0 / 512.0)
                factor = jnp.exp(0.5 * (gn[:, r : r + 1] / (1.0 + mean) - loss_rate))
                for b in range(4):
                    put(base + r, b, factor * linear[b][0], factor * linear[b][1])
                if last_n is not None:
                    leaving = factor * factor * mean
                    updated = 1.0 - recovery * (1.0 - n_here[:, r : r + 1] / (1.0 + leaving))
                    last_n = jnp.where(lane == base + r, updated, last_n)
            return last_n

        def get_e(base, count):
            return e_in[pl.ds(base, count)]

        def put_mid(i, b, re, im):
            mid[i, b, :, 0:128] = re
            mid[i, b, :, 128:256] = im

        def put_out(i, b, re, im):
            e_out[i, b, :, 0:128] = re
            e_out[i, b, :, 128:256] = im

        def get_mid(base, count):
            return mid[pl.ds(base, count)]

        halo_near = halo[other, 0:128, :].reshape(4, 32, 256)

        def one(g, carry):
            base = g * GROUP
            rows_step(get_e, lambda: e_in[base + GROUP], put_mid, base, GROUP, None)
            return carry

        lax.fori_loop(0, ROWS // GROUP - 1, one, 0)
        rows_step(get_e, lambda: halo_near, put_mid, ROWS - GROUP, GROUP, None)

        def edge_row():
            turn_by = 128 - ROWS
            gn = pltpu.roll(gain_n, turn_by, 1)[:, 0:1]
            cs = [pltpu.roll(coef[k], turn_by, 1)[:, 0:1] for k in range(2, 6)]
            x = halo_near[None]
            y = products(x)
            before = e_in[ROWS - 1]
            after = halo[other, 128:256, :].reshape(4, 32, 256)
            linear = []
            power = jnp.zeros((32, 128), F32)
            for b in range(4):
                own = x[0, b]
                spread = (
                    cs[0] * before[b]
                    + cs[1] * after[b]
                    + cs[2] * pltpu.roll(own, 1, 0)
                    + cs[3] * pltpu.roll(own, 31, 0)
                )
                re = y[0, b, :, 0:128] - spread[:, 128:256]
                im = y[0, b, :, 128:256] + spread[:, 0:128]
                power += re * re + im * im
                linear.append((re, im))
            mean = jnp.sum(power, axis=1, keepdims=True) * (1.0 / 512.0)
            factor = jnp.exp(0.5 * (gn / (1.0 + mean) - loss_rate))
            for b in range(4):
                put_mid(ROWS, b, factor * linear[b][0], factor * linear[b][1])

        edge_row()

        def two(g, last_n):
            base = g * GROUP
            return rows_step(get_mid, lambda: mid[base + GROUP], put_out, base, GROUP, last_n)

        last_n = lax.fori_loop(0, ROWS // GROUP, two, jnp.zeros((32, 128), F32))

        @pl.when(keep == 1)
        def _():
            copy = pltpu.make_async_copy(
                e_out.at[pl.ds(keep_row, 2)], taps_out.at[slot], t_sem
            )
            copy.start()
            copy.wait()

        pay[0:128, :] = e_out[ROWS - 1].reshape(128, 256)
        pay[128:256, :] = e_out[ROWS - 2].reshape(128, 256)
        pay[256:288, 0:128] = last_n
        pay[256:288, 128:256] = last_n


def section_call(turn, info, e, halo, msg, coef, w_blocks, taps):
    blocks = len(w_blocks)
    vmem = pl.BlockSpec(memory_space=pltpu.VMEM)
    hbm = pl.BlockSpec(memory_space=pl.ANY)
    n_in = 5 + blocks + 1
    return pl.pallas_call(
        functools.partial(section_kernel, turn, blocks),
        out_shape=(
            jax.ShapeDtypeStruct((ROWS, 4, 32, 256), F32),
            jax.ShapeDtypeStruct((288, 256), F32),
            jax.ShapeDtypeStruct(taps.shape, F32),
        ),
        in_specs=[pl.BlockSpec(memory_space=pltpu.SMEM), vmem, vmem, vmem, vmem]
        + [hbm] * (blocks + 1),
        out_specs=(vmem, vmem, hbm),
        scratch_shapes=[
            pltpu.VMEM((ROWS + 1, 4, 32, 256), F32),
            pltpu.VMEM((16, 48, 256), F32),
            pltpu.VMEM((768, 256), BF16),
            pltpu.VMEM((768, 256), BF16),
            pltpu.SemaphoreType.DMA,
            pltpu.SemaphoreType.DMA,
        ],
        input_output_aliases={n_in - 1: 2},
        compiler_params=pltpu.CompilerParams(vmem_limit_bytes=32 * 1024 * 1024),
        name="section",
    )(info, e, halo, msg, coef, *w_blocks, taps)


def local(input_fields, injection_order, dispersion, coupling, amplifier_gain, inversion):
    seg, row = lax.axis_index("segment"), lax.axis_index("row")
    x, z_lo = seg % 4, seg // 4
    core, y, z_hi = row % 2, (row // 2) % 8, row // 16
    chips = [[2 * k, 2 * k + 1] for k in range(16)]
    rings = [[4 * k + i for i in range(4)] for k in range(4)]
    ahead = [(g, g + 1) for g in range(16) if g % 4 < 3]

    own = jnp.concatenate(
        [inversion[0], amplifier_gain[0], coupling[0, :, 0]], axis=0
    ).reshape(1, 192)
    own = jnp.pad(own, ((0, 7), (0, 64)))
    sent = jnp.concatenate(
        [dispersion[0].reshape(16, 48, 256), jnp.broadcast_to(own[None], (16, 8, 256))], axis=1
    )
    got = lax.all_to_all(sent, "segment", 0, 0)
    w_all = [lax.all_gather(got[4 * k : 4 * k + 4, :48], "segment") for k in range(4)]

    field = lax.dynamic_index_in_dim(input_fields, injection_order[x], 0, keepdims=False)[0]
    field = field.transpose(1, 0, 2).reshape(128, 256)
    rows = lax.all_gather(jnp.concatenate([field, got[:, 48]], axis=0), "row")
    rows = jnp.where(core == 0, rows[: ROWS + 2], jnp.flip(rows[32 - ROWS - 2 :], 0))
    e = rows[:ROWS, :128].reshape(ROWS, 4, 32, 256)
    edge = rows[ROWS:, :128].reshape(256, 256)
    halo = jnp.broadcast_to(jnp.pad(edge, ((0, 32), (0, 0)))[None], (2, 288, 256))
    table = rows[: ROWS + 1, 128:, :192].reshape(ROWS + 1, 16, 6, 32).transpose(1, 2, 3, 0)
    n0, gain, up, down, left, right = (table[:, k] for k in range(6))
    before = jnp.where(core == 0, up, down)
    after = jnp.where(core == 0, down, up)
    at_row = jnp.arange(ROWS + 1)[None, None, :]
    at_col = jnp.arange(32)[None, :, None]
    before = jnp.where(at_row == 0, 0.0, before)
    left = jnp.where(at_col == 0, 0.0, left)
    right = jnp.where(at_col == 31, 0.0, right)
    table = jnp.stack([n0, gain, before, after, left, right], axis=1)
    table = jnp.pad(table, ((0, 0), (0, 0), (0, 0), (0, 128 - ROWS - 1)))

    taps = jnp.zeros((4, 2, 4, 32, 256), F32)
    keep_row = jnp.where(core == 0, 2 * y, 14 - 2 * y)
    turns = 16 + 3 * LAG
    msgs = {}
    for turn in range(turns):
        section = turn - LAG * x
        active = jnp.logical_and(section >= 0, section < 16)
        at = jnp.clip(section, 0, 15)
        keep = active & (at // 4 == z_lo) & (core == z_hi)
        info = jnp.stack(
            [active, at % 4, at // 4, x == 0, core, keep, keep_row, 0 * x]
        ).astype(jnp.int32)
        msg = msgs.pop(turn - LAG, None)
        if msg is None:
            msg = jnp.zeros((2, 32, 256), F32)
        coef = lax.dynamic_index_in_dim(table, at, 0, keepdims=False)
        have = w_all[: min(turn, 15) // 4 + 1]
        e, pay, taps = section_call(turn, info, e, halo, msg, coef, have, taps)
        if turn + 1 < turns:
            halo = lax.all_gather(pay, "row", axis_index_groups=chips)
        if turn + LAG < turns:
            msgs[turn] = lax.ppermute(halo[:, 256:], "segment", ahead)

    both = lax.all_gather(taps, "row", axis_index_groups=chips)
    mine = lax.dynamic_index_in_dim(both, z_hi, 0, keepdims=False)
    mine = lax.dynamic_index_in_dim(
        mine, jnp.where(z_hi == 0, core, 1 - core), 1, keepdims=False
    )
    out = lax.all_to_all(mine, "segment", 0, 0, axis_index_groups=rings)
    return out.transpose(0, 2, 1, 3)[None, :, None]


def solution(mesh):
    return jax.shard_map(
        local,
        mesh=mesh,
        in_specs=(
            P(None, "row", None, None, None),
            P(),
            P("segment", None, None),
            P("segment", None, "row", None),
            P("segment", "row", None),
            P("segment", "row", None),
        ),
        out_specs=P("segment", None, "row", None, None, None),
        check_vma=False,
    )
```

```python
import jax
import jax.numpy as jnp
from jax import lax
from jax.experimental import pallas as pl
from jax.experimental.pallas import tpu as pltpu
from jax.sharding import PartitionSpec as P

STEPS = 2
loss_rate = 0.2
recovery = 0.8
F32 = jnp.float32
BF16 = jnp.bfloat16

ROWS = 16
GROUP = 4
HALF = 384
PAY = 288 + HALF
LAG = 2


def section_kernel(info, e_in, halo, msg, here, taps_in, e_out, pay, taps_out, mid, w_hi, w_lo):
    active, first, core, keep, keep_row, slot = (info[k] for k in range(6))
    lane = lax.broadcasted_iota(jnp.int32, (32, 128), 1)
    other = 1 - core
    coefs = [here[HALF + 16 * k : HALF + 16 * k + 16, :] for k in range(6)]
    coefs = [jnp.concatenate([v[:, 0:128], v[:, 128:256]], axis=0) for v in coefs]
    pay[288:, :] = here[0:HALF, :]

    @pl.when(active == 0)
    def _():
        e_out[...] = e_in[...]
        pay[0:128, :] = e_in[ROWS - 1].reshape(128, 256)
        pay[128:256, :] = e_in[ROWS - 2].reshape(128, 256)
        pay[256:288, :] = jnp.zeros((32, 256), F32)

    @pl.when(active == 1)
    def _():
        for k in range(2):
            w = halo[k, 288 : 288 + HALF, :]
            hi = w.astype(BF16)
            w_hi[k * HALF : (k + 1) * HALF, :] = hi
            w_lo[k * HALF : (k + 1) * HALF, :] = (w - hi.astype(F32)).astype(BF16)

        theirs = pltpu.roll(msg[other, :, 0:128], 1, 1)
        received = jnp.where(lane == ROWS, theirs, msg[core, :, 0:128])
        n = jnp.where(first == 1, coefs[0], received)
        gain_n = coefs[1] * n

        def products(x):
            rows = x.shape[0]
            flat = x.reshape(rows * 4, 32, 256)
            hi = flat.astype(BF16)
            lo = (flat - hi.astype(F32)).astype(BF16)
            zero = jnp.zeros((32, 256), BF16)

            def wide(v):
                parts = []
                for i in range(rows * 4):
                    b = i % 4
                    before = v[i - 1] if b > 0 else zero
                    after = v[i + 1] if b < 3 else zero
                    parts.append(jnp.concatenate([before, v[i], after], axis=1))
                return jnp.concatenate(parts, axis=0)

            hi, lo = wide(hi), wide(lo)
            y = jnp.dot(hi, w_hi[...], preferred_element_type=F32)
            y += jnp.dot(lo, w_hi[...], preferred_element_type=F32)
            y += jnp.dot(hi, w_lo[...], preferred_element_type=F32)
            return y.reshape(rows, 4, 32, 256)

        def rows_step(get, row_before, row_after, dst, base, count, last_n):
            turn_by = (128 - base) % 128 if isinstance(base, int) else lax.rem(128 - base, 128)
            gn, n_here, c_prev, c_next, c_left, c_right = (
                pltpu.roll(v, turn_by, 1) for v in (gain_n, n, *coefs[2:])
            )
            x = get(base, count)
            y = products(x)
            for r in range(count):
                before = row_before if r == 0 else x[r - 1]
                after = row_after if r == count - 1 else x[r + 1]
                cp, cn = c_prev[:, r : r + 1], c_next[:, r : r + 1]
                cl, cr = c_left[:, r : r + 1], c_right[:, r : r + 1]
                linear = []
                power = jnp.zeros((32, 128), F32)
                for b in range(4):
                    own = x[r, b]
                    spread = (
                        cp * before[b]
                        + cn * after[b]
                        + cl * pltpu.roll(own, 1, 0)
                        + cr * pltpu.roll(own, 31, 0)
                    )
                    re = y[r, b, :, 0:128] - spread[:, 128:256]
                    im = y[r, b, :, 128:256] + spread[:, 0:128]
                    power += re * re + im * im
                    linear.append((re, im))
                mean = jnp.sum(power, axis=1, keepdims=True) * (1.0 / 512.0)
                factor = jnp.exp(0.5 * (gn[:, r : r + 1] / (1.0 + mean) - loss_rate))
                for b in range(4):
                    dst[base + r, b, :, 0:128] = factor * linear[b][0]
                    dst[base + r, b, :, 128:256] = factor * linear[b][1]
                if last_n is not None:
                    leaving = factor * factor * mean
                    updated = 1.0 - recovery * (1.0 - n_here[:, r : r + 1] / (1.0 + leaving))
                    last_n = jnp.where(lane == base + r, updated, last_n)
            return last_n

        near = halo[other, 0:128, :].reshape(4, 32, 256)
        far = halo[other, 128:256, :].reshape(4, 32, 256)

        def get_e(base, count):
            return e_in[pl.ds(base, count)]

        def get_mid(base, count):
            return mid[pl.ds(base, count)]

        def one(g, carry):
            base = g * GROUP
            rows_step(get_e, e_in[jnp.maximum(base - 1, 0)], e_in[base + GROUP], mid, base, GROUP, None)
            return carry

        def two(g, last_n):
            base = g * GROUP
            before = mid[jnp.maximum(base - 1, 0)]
            return rows_step(get_mid, before, mid[base + GROUP], e_out, base, GROUP, last_n)

        last = ROWS - GROUP
        lax.fori_loop(0, ROWS // GROUP - 1, one, 0)
        rows_step(get_e, e_in[last - 1], near, mid, last, GROUP, None)
        rows_step(lambda *_: near[None], e_in[ROWS - 1], far, mid, ROWS, 1, None)
        last_n = lax.fori_loop(0, ROWS // GROUP, two, jnp.zeros((32, 128), F32))

        @pl.when(keep == 1)
        def _():
            taps_out[slot] = e_out[pl.ds(keep_row, 2)]

        pay[0:128, :] = e_out[ROWS - 1].reshape(128, 256)
        pay[128:256, :] = e_out[ROWS - 2].reshape(128, 256)
        pay[256:288, 0:128] = last_n
        pay[256:288, 128:256] = last_n


def section_call(info, e, halo, msg, here, taps):
    vmem = pl.BlockSpec(memory_space=pltpu.VMEM)
    return pl.pallas_call(
        section_kernel,
        out_shape=(
            jax.ShapeDtypeStruct((ROWS, 4, 32, 256), F32),
            jax.ShapeDtypeStruct((PAY, 256), F32),
            jax.ShapeDtypeStruct(taps.shape, F32),
        ),
        in_specs=[pl.BlockSpec(memory_space=pltpu.SMEM)] + [vmem] * 5,
        out_specs=(vmem, vmem, vmem),
        scratch_shapes=[
            pltpu.VMEM((ROWS + 1, 4, 32, 256), F32),
            pltpu.VMEM((768, 256), BF16),
            pltpu.VMEM((768, 256), BF16),
        ],
        input_output_aliases={5: 2},
        compiler_params=pltpu.CompilerParams(vmem_limit_bytes=40 * 1024 * 1024),
        name="section",
    )(info, e, halo, msg, here, taps)


def local(input_fields, injection_order, dispersion, coupling, amplifier_gain, inversion):
    seg, row = lax.axis_index("segment"), lax.axis_index("row")
    x, z_lo = seg % 4, seg // 4
    core, y, z_hi = row % 2, (row // 2) % 8, row // 16
    chips = [[2 * k, 2 * k + 1] for k in range(16)]
    rings = [[4 * k + i for i in range(4)] for k in range(4)]
    columns = [[16 * h + 2 * k + c for k in range(8)] for h in range(2) for c in range(2)]
    across = [(17 * h + 2 * k, 16 * (1 - h) + 2 * k + h) for h in range(2) for k in range(8)]
    ahead = [(g, g + 1) for g in range(16) if g % 4 < 3]

    half = lax.dynamic_slice_in_dim(dispersion[0], HALF * core, HALF, 0)
    w_all = lax.all_gather(half, "segment")

    own = jnp.concatenate([inversion[0], amplifier_gain[0], coupling[0, :, 0]], axis=0)
    own = jnp.pad(own.reshape(1, 192), ((0, 0), (0, 64)))
    row_coefs = lax.all_to_all(jnp.broadcast_to(own[None], (16, 1, 256)), "segment", 0, 0)[:, 0]

    field = lax.dynamic_index_in_dim(input_fields, injection_order[x], 0, keepdims=False)[0]
    field = field.transpose(1, 0, 2).reshape(128, 256)
    pair = lax.all_gather(
        jnp.concatenate([field, row_coefs], axis=0), "row", axis_index_groups=chips
    )
    pair = jnp.where(core == z_hi, pair, lax.ppermute(pair, "row", across))
    rows = lax.all_to_all(
        jnp.broadcast_to(pair[None], (8, 2, 144, 256)), "row", 0, 0, axis_index_groups=columns
    ).reshape(ROWS, 144, 256)
    rows = jnp.where(core == 0, rows, jnp.flip(rows, 0))
    e = rows[:, :128].reshape(ROWS, 4, 32, 256)
    sibling = lax.all_gather(rows[ROWS - 1, 128:], "row", axis_index_groups=chips)
    sibling = lax.dynamic_index_in_dim(sibling, 1 - core, 0)
    table = jnp.concatenate([rows[:, 128:], sibling], axis=0)[:, :, :192]
    table = table.reshape(ROWS + 1, 16, 6, 32).transpose(1, 2, 3, 0)
    n0, gain, up, down, left, right = (table[:, k] for k in range(6))
    before = jnp.where(core == 0, up, down)
    after = jnp.where(core == 0, down, up)
    at_row = jnp.arange(ROWS + 1)[None, None, :]
    at_col = jnp.arange(32)[None, :, None]
    before = jnp.where(at_row == 0, 0.0, before)
    left = jnp.where(at_col == 0, 0.0, left)
    right = jnp.where(at_col == 31, 0.0, right)
    table = jnp.stack([n0, gain, before, after, left, right], axis=1)
    table = jnp.pad(table, ((0, 0), (0, 0), (0, 0), (0, 128 - ROWS - 1)))
    table = jnp.concatenate([table[:, :, :16], table[:, :, 16:]], axis=3).reshape(16, 96, 256)

    turns = 16 + 3 * LAG

    def section_at(turn):
        return jnp.clip(turn - LAG * x, 0, 15)

    def here_at(turn):
        w = lax.dynamic_index_in_dim(w_all, section_at(turn + 1), 0, keepdims=False)
        coef = lax.dynamic_index_in_dim(table, section_at(turn), 0, keepdims=False)
        return jnp.concatenate([w, coef], axis=0)

    first_pay = jnp.concatenate(
        [e[ROWS - 1].reshape(128, 256), e[ROWS - 2].reshape(128, 256), jnp.zeros((32, 256), F32), w_all[0]],
        axis=0,
    )
    halo = lax.all_gather(first_pay, "row", axis_index_groups=chips)
    taps = jnp.zeros((4, 2, 4, 32, 256), F32)
    keep_row = jnp.where(core == 0, 2 * y, 14 - 2 * y)
    msgs = {}
    for turn in range(turns):
        section = turn - LAG * x
        active = jnp.logical_and(section >= 0, section < 16)
        at = section_at(turn)
        keep = active & (at // 4 == z_lo) & (core == z_hi)
        info = jnp.stack([active, x == 0, core, keep, keep_row, at % 4]).astype(jnp.int32)
        msg = msgs.pop(turn - LAG, None)
        if msg is None:
            msg = jnp.zeros((2, 32, 256), F32)
        e, pay, taps = section_call(info, e, halo, msg, here_at(turn), taps)
        if turn + 1 < turns:
            halo = lax.all_gather(pay, "row", axis_index_groups=chips)
        if turn + LAG < turns:
            msgs[turn] = lax.ppermute(halo[:, 256:288], "segment", ahead)

    taps = jnp.where(z_hi == 0, taps, jnp.flip(taps, 1)).swapaxes(0, 1)
    both = lax.all_to_all(taps, "row", 0, 0, axis_index_groups=chips)
    mine = lax.dynamic_index_in_dim(both, z_hi, 0, keepdims=False)
    out = lax.all_to_all(mine, "segment", 0, 0, axis_index_groups=rings)
    return out.transpose(0, 2, 1, 3)[None, :, None]


def solution(mesh):
    return jax.shard_map(
        local,
        mesh=mesh,
        in_specs=(
            P(None, "row", None, None, None),
            P(),
            P("segment", None, None),
            P("segment", None, "row", None),
            P("segment", "row", None),
            P("segment", "row", None),
        ),
        out_specs=P("segment", None, "row", None, None, None),
        check_vma=False,
    )
```

```python
import jax
import jax.numpy as jnp
from jax import lax
from jax.experimental import pallas as pl
from jax.experimental.pallas import tpu as pltpu
from jax.sharding import PartitionSpec as P

STEPS = 2
loss_rate = 0.2
recovery = 0.8
F32 = jnp.float32
BF16 = jnp.bfloat16

ROWS = 16
GROUP = 8
PAY = 288
LAG = 2


def section_kernel(
    count, ids, e_in, halo, msg, table, w_all, taps_in,
    count_out, e_out, pay, taps_out,
    mid, w_f32, w_hi, w_lo, coef, w_sem, c_sem, t_sem,
):
    turn = count[0]
    field, z_lo, core, half_here, keep_row = (ids[k] for k in range(5))
    section = turn - LAG * field
    active = jnp.logical_and(section >= 0, section < 16)
    at = jnp.clip(section, 0, 15)
    keep = jnp.logical_and(active, jnp.logical_and(at // 4 == z_lo, half_here == core))
    slot = lax.rem(at, 4)
    count_out[0] = turn + 1
    lane = lax.broadcasted_iota(jnp.int32, (32, 128), 1)
    other = 1 - core

    @pl.when(jnp.logical_not(active))
    def _():
        e_out[...] = e_in[...]
        pay[0:128, :] = e_in[ROWS - 1].reshape(128, 256)
        pay[128:256, :] = e_in[ROWS - 2].reshape(128, 256)
        pay[256:288, :] = jnp.zeros((32, 256), F32)

    @pl.when(active)
    def _():
        w_copy = pltpu.make_async_copy(w_all.at[at], w_f32, w_sem)
        c_copy = pltpu.make_async_copy(table.at[at], coef, c_sem)
        w_copy.start()
        c_copy.start()
        w_copy.wait()
        c_copy.wait()
        w = w_f32[...]
        hi = w.astype(BF16)
        w_hi[...] = hi
        w_lo[...] = (w - hi.astype(F32)).astype(BF16)
        coefs = [coef[k] for k in range(6)]

        theirs = pltpu.roll(msg[other, :, 0:128], 1, 1)
        received = jnp.where(lane == ROWS, theirs, msg[core, :, 0:128])
        n = jnp.where(field == 0, coefs[0], received)
        gain_n = coefs[1] * n

        def products(x):
            rows = x.shape[0]
            flat = x.reshape(rows * 4, 32, 256)
            hi = flat.astype(BF16)
            lo = (flat - hi.astype(F32)).astype(BF16)
            zero = jnp.zeros((32, 256), BF16)

            def wide(v):
                parts = []
                for i in range(rows * 4):
                    b = i % 4
                    before = v[i - 1] if b > 0 else zero
                    after = v[i + 1] if b < 3 else zero
                    parts.append(jnp.concatenate([before, v[i], after], axis=1))
                return jnp.concatenate(parts, axis=0)

            hi, lo = wide(hi), wide(lo)
            y = jnp.dot(hi, w_hi[...], preferred_element_type=F32)
            y += jnp.dot(lo, w_hi[...], preferred_element_type=F32)
            y += jnp.dot(hi, w_lo[...], preferred_element_type=F32)
            return y.reshape(rows, 4, 32, 256)

        def rows_step(get, row_before, row_after, dst, base, count, last_n):
            turn_by = (128 - base) % 128 if isinstance(base, int) else lax.rem(128 - base, 128)
            gn, n_here, c_prev, c_next, c_left, c_right = (
                pltpu.roll(v, turn_by, 1) for v in (gain_n, n, *coefs[2:])
            )
            x = get(base, count)
            y = products(x)
            for r in range(count):
                before = row_before if r == 0 else x[r - 1]
                after = row_after if r == count - 1 else x[r + 1]
                cp, cn = c_prev[:, r : r + 1], c_next[:, r : r + 1]
                cl, cr = c_left[:, r : r + 1], c_right[:, r : r + 1]
                linear = []
                power = jnp.zeros((32, 128), F32)
                for b in range(4):
                    own = x[r, b]
                    spread = (
                        cp * before[b]
                        + cn * after[b]
                        + cl * pltpu.roll(own, 1, 0)
                        + cr * pltpu.roll(own, 31, 0)
                    )
                    re = y[r, b, :, 0:128] - spread[:, 128:256]
                    im = y[r, b, :, 128:256] + spread[:, 0:128]
                    power += re * re + im * im
                    linear.append((re, im))
                mean = jnp.sum(power, axis=1, keepdims=True) * (1.0 / 512.0)
                factor = jnp.exp(0.5 * (gn[:, r : r + 1] / (1.0 + mean) - loss_rate))
                for b in range(4):
                    dst[base + r, b, :, 0:128] = factor * linear[b][0]
                    dst[base + r, b, :, 128:256] = factor * linear[b][1]
                if last_n is not None:
                    leaving = factor * factor * mean
                    updated = 1.0 - recovery * (1.0 - n_here[:, r : r + 1] / (1.0 + leaving))
                    last_n = jnp.where(lane == base + r, updated, last_n)
            return last_n

        near = halo[other, 0:128, :].reshape(4, 32, 256)
        far = halo[other, 128:256, :].reshape(4, 32, 256)

        def get_e(base, count):
            return e_in[pl.ds(base, count)]

        def get_mid(base, count):
            return mid[pl.ds(base, count)]

        def one(g, carry):
            base = g * GROUP
            rows_step(get_e, e_in[jnp.maximum(base - 1, 0)], e_in[base + GROUP], mid, base, GROUP, None)
            return carry

        def two(g, last_n):
            base = g * GROUP
            before = mid[jnp.maximum(base - 1, 0)]
            return rows_step(get_mid, before, mid[base + GROUP], e_out, base, GROUP, last_n)

        last = ROWS - GROUP
        lax.fori_loop(0, ROWS // GROUP - 1, one, 0)
        rows_step(get_e, e_in[last - 1], near, mid, last, GROUP, None)
        rows_step(lambda *_: near[None], e_in[ROWS - 1], far, mid, ROWS, 1, None)
        last_n = lax.fori_loop(0, ROWS // GROUP, two, jnp.zeros((32, 128), F32))

        @pl.when(keep)
        def _():
            t_copy = pltpu.make_async_copy(e_out.at[pl.ds(keep_row, 2)], taps_out.at[slot], t_sem)
            t_copy.start()
            t_copy.wait()

        pay[0:128, :] = e_out[ROWS - 1].reshape(128, 256)
        pay[128:256, :] = e_out[ROWS - 2].reshape(128, 256)
        pay[256:288, 0:128] = last_n
        pay[256:288, 128:256] = last_n


def section_call(count, ids, e, halo, msg, table, w_all, taps):
    vmem = pl.BlockSpec(memory_space=pltpu.VMEM)
    smem = pl.BlockSpec(memory_space=pltpu.SMEM)
    hbm = pl.BlockSpec(memory_space=pl.ANY)
    return pl.pallas_call(
        section_kernel,
        out_shape=(
            jax.ShapeDtypeStruct((1,), jnp.int32),
            jax.ShapeDtypeStruct((ROWS, 4, 32, 256), F32),
            jax.ShapeDtypeStruct((PAY, 256), F32),
            jax.ShapeDtypeStruct(taps.shape, F32),
        ),
        in_specs=[smem, smem, vmem, vmem, vmem, hbm, hbm, hbm],
        out_specs=(smem, vmem, vmem, hbm),
        scratch_shapes=[
            pltpu.VMEM((ROWS + 1, 4, 32, 256), F32),
            pltpu.VMEM((768, 256), F32),
            pltpu.VMEM((768, 256), BF16),
            pltpu.VMEM((768, 256), BF16),
            pltpu.VMEM((6, 32, 128), F32),
            pltpu.SemaphoreType.DMA,
            pltpu.SemaphoreType.DMA,
            pltpu.SemaphoreType.DMA,
        ],
        input_output_aliases={7: 3},
        compiler_params=pltpu.CompilerParams(vmem_limit_bytes=32 * 1024 * 1024),
        cost_estimate=pl.CostEstimate(
            flops=33 * 3 * 2 * 128 * 768 * 256, bytes_accessed=8 << 20, transcendentals=0
        ),
        name="section",
    )(count, ids, e, halo, msg, table, w_all, taps)


def local(input_fields, injection_order, dispersion, coupling, amplifier_gain, inversion):
    seg, row = lax.axis_index("segment"), lax.axis_index("row")
    x, z_lo = seg % 4, seg // 4
    core, y, z_hi = row % 2, (row // 2) % 8, row // 16
    chips = [[2 * k, 2 * k + 1] for k in range(16)]
    rings = [[4 * k + i for i in range(4)] for k in range(4)]
    columns = [[16 * h + 2 * k + c for k in range(8)] for h in range(2) for c in range(2)]
    across = [(17 * h + 2 * k, 16 * (1 - h) + 2 * k + h) for h in range(2) for k in range(8)]
    ahead = [(g, g + 1) for g in range(16) if g % 4 < 3]

    w_all = lax.all_gather(dispersion[0], "segment")

    own = jnp.concatenate([inversion[0], amplifier_gain[0], coupling[0, :, 0]], axis=0)
    own = jnp.pad(own.reshape(1, 192), ((0, 0), (0, 64)))
    row_coefs = lax.all_to_all(jnp.broadcast_to(own[None], (16, 1, 256)), "segment", 0, 0)[:, 0]

    field = lax.dynamic_index_in_dim(input_fields, injection_order[x], 0, keepdims=False)[0]
    field = field.transpose(1, 0, 2).reshape(128, 256)
    pair = lax.all_gather(
        jnp.concatenate([field, row_coefs], axis=0), "row", axis_index_groups=chips
    )
    pair = jnp.where(core == z_hi, pair, lax.ppermute(pair, "row", across))
    rows = lax.all_to_all(
        jnp.broadcast_to(pair[None], (8, 2, 144, 256)), "row", 0, 0, axis_index_groups=columns
    ).reshape(ROWS, 144, 256)
    rows = jnp.where(core == 0, rows, jnp.flip(rows, 0))
    e = rows[:, :128].reshape(ROWS, 4, 32, 256)
    sibling = lax.all_gather(rows[ROWS - 1, 128:], "row", axis_index_groups=chips)
    sibling = lax.dynamic_index_in_dim(sibling, 1 - core, 0)
    table = jnp.concatenate([rows[:, 128:], sibling], axis=0)[:, :, :192]
    table = table.reshape(ROWS + 1, 16, 6, 32).transpose(1, 2, 3, 0)
    n0, gain, up, down, left, right = (table[:, k] for k in range(6))
    before = jnp.where(core == 0, up, down)
    after = jnp.where(core == 0, down, up)
    at_row = jnp.arange(ROWS + 1)[None, None, :]
    at_col = jnp.arange(32)[None, :, None]
    before = jnp.where(at_row == 0, 0.0, before)
    left = jnp.where(at_col == 0, 0.0, left)
    right = jnp.where(at_col == 31, 0.0, right)
    table = jnp.stack([n0, gain, before, after, left, right], axis=1)
    table = jnp.pad(table, ((0, 0), (0, 0), (0, 0), (0, 128 - ROWS - 1)))

    pay = jnp.concatenate(
        [e[ROWS - 1].reshape(128, 256), e[ROWS - 2].reshape(128, 256), jnp.zeros((32, 256), F32)], axis=0
    )
    halo = lax.all_gather(pay, "row", axis_index_groups=chips)
    taps = jnp.zeros((4, 2, 4, 32, 256), F32)
    keep_row = jnp.where(core == 0, 2 * y, 14 - 2 * y)
    ids = jnp.stack([x, z_lo, core, z_hi, keep_row]).astype(jnp.int32)

    def two_turns(_, carry):
        count, e, halo, msg, taps = carry
        for _ in range(2):
            coming = lax.ppermute(halo[:, 256:], "segment", ahead)
            count, e, pay, taps = section_call(count, ids, e, halo, msg, table, w_all, taps)
            halo = lax.all_gather(pay, "row", axis_index_groups=chips)
            msg = coming
        return count, e, halo, msg, taps

    start = (jnp.zeros((1,), jnp.int32), e, halo, jnp.zeros((2, 32, 256), F32), taps)
    taps = lax.fori_loop(0, (16 + 3 * LAG) // 2, two_turns, start)[4]

    taps = jnp.where(z_hi == 0, taps, jnp.flip(taps, 1)).swapaxes(0, 1)
    both = lax.all_to_all(taps, "row", 0, 0, axis_index_groups=chips)
    mine = lax.dynamic_index_in_dim(both, z_hi, 0, keepdims=False)
    out = lax.all_to_all(mine, "segment", 0, 0, axis_index_groups=rings)
    return out.transpose(0, 2, 1, 3)[None, :, None]


def solution(mesh):
    return jax.shard_map(
        local,
        mesh=mesh,
        in_specs=(
            P(None, "row", None, None, None),
            P(),
            P("segment", None, None),
            P("segment", None, "row", None),
            P("segment", "row", None),
            P("segment", "row", None),
        ),
        out_specs=P("segment", None, "row", None, None, None),
        check_vma=False,
    )
```

```python
import jax
import jax.numpy as jnp
from jax import lax
from jax.experimental import pallas as pl
from jax.experimental.pallas import tpu as pltpu
from jax.sharding import PartitionSpec as P

STEPS = 2
loss_rate = 0.2
recovery = 0.8
F32 = jnp.float32
BF16 = jnp.bfloat16

ROWS = 16
GROUP = 16
PAY = 288
LAG = 2


def section_kernel(
    count, ids, e_in, halo, msg, table, w_all, taps_in,
    count_out, e_out, pay, taps_out,
    mid, w_f32, w_hi, w_lo, coef, w_sem, c_sem, t_sem,
):
    turn = count[0]
    field, z_lo, core, half_here, keep_row = (ids[k] for k in range(5))
    section = turn - LAG * field
    active = jnp.logical_and(section >= 0, section < 16)
    at = jnp.clip(section, 0, 15)
    keep = jnp.logical_and(active, jnp.logical_and(at // 4 == z_lo, half_here == core))
    slot = lax.rem(at, 4)
    count_out[0] = turn + 1
    lane = lax.broadcasted_iota(jnp.int32, (32, 128), 1)
    other = 1 - core

    @pl.when(jnp.logical_not(active))
    def _():
        e_out[...] = e_in[...]
        pay[0:128, :] = e_in[ROWS - 1].reshape(128, 256)
        pay[128:256, :] = e_in[ROWS - 2].reshape(128, 256)
        pay[256:288, :] = jnp.zeros((32, 256), F32)

    @pl.when(active)
    def _():
        w_copy = pltpu.make_async_copy(w_all.at[at], w_f32, w_sem)
        c_copy = pltpu.make_async_copy(table.at[at], coef, c_sem)
        w_copy.start()
        c_copy.start()
        w_copy.wait()
        c_copy.wait()
        w = w_f32[...]
        hi = w.astype(BF16)
        w_hi[...] = hi
        w_lo[...] = (w - hi.astype(F32)).astype(BF16)
        coefs = [coef[k] for k in range(6)]

        theirs = pltpu.roll(msg[other, :, 0:128], 1, 1)
        received = jnp.where(lane == ROWS, theirs, msg[core, :, 0:128])
        n = jnp.where(field == 0, coefs[0], received)
        gain_n = coefs[1] * n

        def products(x):
            rows = x.shape[0]
            flat = x.reshape(rows * 4, 32, 256)
            hi = flat.astype(BF16)
            lo = (flat - hi.astype(F32)).astype(BF16)
            zero = jnp.zeros((32, 256), BF16)

            def wide(v):
                parts = []
                for i in range(rows * 4):
                    b = i % 4
                    before = v[i - 1] if b > 0 else zero
                    after = v[i + 1] if b < 3 else zero
                    parts.append(jnp.concatenate([before, v[i], after], axis=1))
                return jnp.concatenate(parts, axis=0)

            hi, lo = wide(hi), wide(lo)
            y = jnp.dot(hi, w_hi[...], preferred_element_type=F32)
            y += jnp.dot(lo, w_hi[...], preferred_element_type=F32)
            y += jnp.dot(hi, w_lo[...], preferred_element_type=F32)
            return y.reshape(rows, 4, 32, 256)

        def rows_step(get, row_before, row_after, dst, base, count, last_n):
            turn_by = (128 - base) % 128 if isinstance(base, int) else lax.rem(128 - base, 128)
            gn, n_here, c_prev, c_next, c_left, c_right = (
                pltpu.roll(v, turn_by, 1) for v in (gain_n, n, *coefs[2:])
            )
            x = get(base, count)
            y = products(x)
            for r in range(count):
                before = row_before if r == 0 else x[r - 1]
                after = row_after if r == count - 1 else x[r + 1]
                cp, cn = c_prev[:, r : r + 1], c_next[:, r : r + 1]
                cl, cr = c_left[:, r : r + 1], c_right[:, r : r + 1]
                linear = []
                power = jnp.zeros((32, 128), F32)
                for b in range(4):
                    own = x[r, b]
                    spread = (
                        cp * before[b]
                        + cn * after[b]
                        + cl * pltpu.roll(own, 1, 0)
                        + cr * pltpu.roll(own, 31, 0)
                    )
                    re = y[r, b, :, 0:128] - spread[:, 128:256]
                    im = y[r, b, :, 128:256] + spread[:, 0:128]
                    power += re * re + im * im
                    linear.append((re, im))
                mean = jnp.sum(power, axis=1, keepdims=True) * (1.0 / 512.0)
                factor = jnp.exp(0.5 * (gn[:, r : r + 1] / (1.0 + mean) - loss_rate))
                for b in range(4):
                    dst[base + r, b, :, 0:128] = factor * linear[b][0]
                    dst[base + r, b, :, 128:256] = factor * linear[b][1]
                if last_n is not None:
                    leaving = factor * factor * mean
                    updated = 1.0 - recovery * (1.0 - n_here[:, r : r + 1] / (1.0 + leaving))
                    last_n = jnp.where(lane == base + r, updated, last_n)
            return last_n

        near = halo[other, 0:128, :].reshape(4, 32, 256)
        far = halo[other, 128:256, :].reshape(4, 32, 256)

        def get_e(base, count):
            return e_in[pl.ds(base, count)]

        def get_mid(base, count):
            return mid[pl.ds(base, count)]

        def one(g, carry):
            base = g * GROUP
            rows_step(get_e, e_in[jnp.maximum(base - 1, 0)], e_in[base + GROUP], mid, base, GROUP, None)
            return carry

        def two(g, last_n):
            base = g * GROUP
            before = mid[jnp.maximum(base - 1, 0)]
            return rows_step(get_mid, before, mid[base + GROUP], e_out, base, GROUP, last_n)

        last = ROWS - GROUP
        if last:
            lax.fori_loop(0, ROWS // GROUP - 1, one, 0)
        rows_step(get_e, e_in[max(last - 1, 0)], near, mid, last, GROUP, None)
        rows_step(lambda *_: near[None], e_in[ROWS - 1], far, mid, ROWS, 1, None)
        last_n = lax.fori_loop(0, ROWS // GROUP, two, jnp.zeros((32, 128), F32))

        @pl.when(keep)
        def _():
            t_copy = pltpu.make_async_copy(e_out.at[pl.ds(keep_row, 2)], taps_out.at[slot], t_sem)
            t_copy.start()
            t_copy.wait()

        pay[0:128, :] = e_out[ROWS - 1].reshape(128, 256)
        pay[128:256, :] = e_out[ROWS - 2].reshape(128, 256)
        pay[256:288, 0:128] = last_n
        pay[256:288, 128:256] = last_n


def section_call(count, ids, e, halo, msg, table, w_all, taps):
    vmem = pl.BlockSpec(memory_space=pltpu.VMEM)
    smem = pl.BlockSpec(memory_space=pltpu.SMEM)
    hbm = pl.BlockSpec(memory_space=pl.ANY)
    return pl.pallas_call(
        section_kernel,
        out_shape=(
            jax.ShapeDtypeStruct((1,), jnp.int32),
            jax.ShapeDtypeStruct((ROWS, 4, 32, 256), F32),
            jax.ShapeDtypeStruct((PAY, 256), F32),
            jax.ShapeDtypeStruct(taps.shape, F32),
        ),
        in_specs=[smem, smem, vmem, vmem, vmem, hbm, hbm, hbm],
        out_specs=(smem, vmem, vmem, hbm),
        scratch_shapes=[
            pltpu.VMEM((ROWS + 1, 4, 32, 256), F32),
            pltpu.VMEM((768, 256), F32),
            pltpu.VMEM((768, 256), BF16),
            pltpu.VMEM((768, 256), BF16),
            pltpu.VMEM((6, 32, 128), F32),
            pltpu.SemaphoreType.DMA,
            pltpu.SemaphoreType.DMA,
            pltpu.SemaphoreType.DMA,
        ],
        input_output_aliases={7: 3},
        compiler_params=pltpu.CompilerParams(vmem_limit_bytes=32 * 1024 * 1024),
        cost_estimate=pl.CostEstimate(
            flops=33 * 3 * 2 * 128 * 768 * 256, bytes_accessed=8 << 20, transcendentals=0
        ),
        name="section",
    )(count, ids, e, halo, msg, table, w_all, taps)


def local(input_fields, injection_order, dispersion, coupling, amplifier_gain, inversion):
    seg, row = lax.axis_index("segment"), lax.axis_index("row")
    x, z_lo = seg % 4, seg // 4
    core, y, z_hi = row % 2, (row // 2) % 8, row // 16
    chips = [[2 * k, 2 * k + 1] for k in range(16)]
    rings = [[4 * k + i for i in range(4)] for k in range(4)]
    columns = [[16 * h + 2 * k + c for k in range(8)] for h in range(2) for c in range(2)]
    across = [(17 * h + 2 * k, 16 * (1 - h) + 2 * k + h) for h in range(2) for k in range(8)]
    ahead = [(g, g + 1) for g in range(16) if g % 4 < 3]

    w_all = lax.all_gather(dispersion[0], "segment")

    own = jnp.concatenate([inversion[0], amplifier_gain[0], coupling[0, :, 0]], axis=0)
    own = jnp.pad(own.reshape(1, 192), ((0, 0), (0, 64)))
    row_coefs = lax.all_to_all(jnp.broadcast_to(own[None], (16, 1, 256)), "segment", 0, 0)[:, 0]

    field = lax.dynamic_index_in_dim(input_fields, injection_order[x], 0, keepdims=False)[0]
    field = field.transpose(1, 0, 2).reshape(128, 256)
    pair = lax.all_gather(
        jnp.concatenate([field, row_coefs], axis=0), "row", axis_index_groups=chips
    )
    pair = jnp.where(core == z_hi, pair, lax.ppermute(pair, "row", across))
    rows = lax.all_to_all(
        jnp.broadcast_to(pair[None], (8, 2, 144, 256)), "row", 0, 0, axis_index_groups=columns
    ).reshape(ROWS, 144, 256)
    rows = jnp.where(core == 0, rows, jnp.flip(rows, 0))
    e = rows[:, :128].reshape(ROWS, 4, 32, 256)
    sibling = lax.all_gather(rows[ROWS - 1, 128:], "row", axis_index_groups=chips)
    sibling = lax.dynamic_index_in_dim(sibling, 1 - core, 0)
    table = jnp.concatenate([rows[:, 128:], sibling], axis=0)[:, :, :192]
    table = table.reshape(ROWS + 1, 16, 6, 32).transpose(1, 2, 3, 0)
    n0, gain, up, down, left, right = (table[:, k] for k in range(6))
    before = jnp.where(core == 0, up, down)
    after = jnp.where(core == 0, down, up)
    at_row = jnp.arange(ROWS + 1)[None, None, :]
    at_col = jnp.arange(32)[None, :, None]
    before = jnp.where(at_row == 0, 0.0, before)
    left = jnp.where(at_col == 0, 0.0, left)
    right = jnp.where(at_col == 31, 0.0, right)
    table = jnp.stack([n0, gain, before, after, left, right], axis=1)
    table = jnp.pad(table, ((0, 0), (0, 0), (0, 0), (0, 128 - ROWS - 1)))

    pay = jnp.concatenate(
        [e[ROWS - 1].reshape(128, 256), e[ROWS - 2].reshape(128, 256), jnp.zeros((32, 256), F32)], axis=0
    )
    halo = lax.all_gather(pay, "row", axis_index_groups=chips)
    taps = jnp.zeros((4, 2, 4, 32, 256), F32)
    keep_row = jnp.where(core == 0, 2 * y, 14 - 2 * y)
    ids = jnp.stack([x, z_lo, core, z_hi, keep_row]).astype(jnp.int32)

    def two_turns(_, carry):
        count, e, halo, msg, taps = carry
        for _ in range(2):
            coming = lax.ppermute(halo[:, 256:], "segment", ahead)
            count, e, pay, taps = section_call(count, ids, e, halo, msg, table, w_all, taps)
            halo = lax.all_gather(pay, "row", axis_index_groups=chips)
            msg = coming
        return count, e, halo, msg, taps

    start = (jnp.zeros((1,), jnp.int32), e, halo, jnp.zeros((2, 32, 256), F32), taps)
    taps = lax.fori_loop(0, (16 + 3 * LAG) // 2, two_turns, start)[4]

    taps = jnp.where(z_hi == 0, taps, jnp.flip(taps, 1)).swapaxes(0, 1)
    both = lax.all_to_all(taps, "row", 0, 0, axis_index_groups=chips)
    mine = lax.dynamic_index_in_dim(both, z_hi, 0, keepdims=False)
    out = lax.all_to_all(mine, "segment", 0, 0, axis_index_groups=rings)
    return out.transpose(0, 2, 1, 3)[None, :, None]


def solution(mesh):
    return jax.shard_map(
        local,
        mesh=mesh,
        in_specs=(
            P(None, "row", None, None, None),
            P(),
            P("segment", None, None),
            P("segment", None, "row", None),
            P("segment", "row", None),
            P("segment", "row", None),
        ),
        out_specs=P("segment", None, "row", None, None, None),
        check_vma=False,
    )
```
